128 devices in a mesh: row: 8 (over x_lo, z), col: 16 (over x_hi, y, core).
Axes of the slice: x: 4 (x_hi: 2, x_lo: 2; x = x_hi * 2 + x_lo), y: 4, z: 4, core: 2. Of those that a mesh axis runs over, the one named last changes fastest.
Arguments:
- start_basis: float32 [65536, 256], P(('row', 'col')), may hold values from -6 to 6
- affinity_tiles: bfloat16 [18432, 256, 256], P(('row', 'col')), may hold values from -0.046875 to 0.046875
- tile_rows: int32 [18432], P(('row', 'col')), may hold values from 0 to 15, as said below
- tile_cols: int32 [18432], P(('row', 'col')), may hold values from 0 to 31, as said below
- live_tiles: int32 [128], P(('row', 'col')), may hold values from 32 to 144, as said below
- filter_center: float32 [1], replicated, may hold values from -0.3 to 0.3
- filter_radius: float32 [1], replicated, may hold values from 0.6 to 1.2
Outputs:
- filtered: float32 [65536, 256], P(('row', 'col'))
The draws below stay inside these ranges and needn't reach their ends.
Inputs may be any that keep to these rules, and one draw needn't show every extreme that they name: `tile_rows`: every value is a tile row of a device's row group; on every device the first 8 * 2 slots name each tile row once. `tile_cols`: every value is a tile column of a device's column group; on every device the first 16 * 2 slots name each tile column once. `live_tiles`: some device uses all 144 slots.
All inputs are finite; a program needn't handle non-finite values.
Results may differ from the reference program's by a relative error of at most 0.0003.
Values sent between devices are 32-bit elements; how exact they have to be, the bound alone decides.
A program may use at most 128 MiB of HBM per device.

```python
import jax
import jax.numpy as jnp
from jax import lax

K = 256
BLK = 256
PIECE_TILES = 2
PIECE = 512
NT = 144
ROWS = 65536
N_ROW = 8
N_COL = 16
DEVICES = 128


def cover_draw(seed_key, extent):
    first_key, second_key = jax.random.split(seed_key)
    device_keys = jax.random.split(first_key, DEVICES)
    covered = jax.vmap(lambda subkey: jax.random.permutation(subkey, extent))(device_keys)
    extra = jax.random.randint(second_key, (DEVICES, NT - extent), 0, extent)
    return jnp.concatenate([covered.astype(jnp.int32), extra.astype(jnp.int32)], axis=1).reshape(-1)


def draw_tile_rows(key, part):
    key = jax.random.fold_in(key, 11)
    return cover_draw(key, N_ROW * PIECE_TILES)


def draw_tile_cols(key, part):
    key = jax.random.fold_in(key, 12)
    return cover_draw(key, N_COL * PIECE_TILES)


def draw_live_tiles(key, part):
    key = jax.random.fold_in(key, 13)
    first_key, second_key = jax.random.split(key)
    lowest = max(N_ROW, N_COL) * PIECE_TILES
    counts = jax.random.randint(first_key, (DEVICES,), lowest, NT + 1)
    fullest = jax.random.randint(second_key, (), 0, DEVICES)
    return jnp.where(jnp.arange(DEVICES) == fullest, NT, counts).astype(jnp.int32)


def steps_of(stream_key, dims, cuts, low, largest):
    def one(dim, shards_of):
        heights = jax.random.uniform(jax.random.fold_in(jax.random.fold_in(stream_key, 6), dim), (shards_of,), jnp.float32, low / len(cuts), largest / len(cuts))
        return jnp.repeat(jnp.exp(heights), dims[dim] // shards_of).reshape((-1,) + (1,) * (len(dims) - dim - 1))

    loudness = one(*cuts[0])
    for cut in cuts[1:]:
        loudness = loudness * one(*cut)
    return loudness


def centred(key, shape, deviation, bound, cuts=(), kind=jnp.bfloat16):
    factor_of = steps_of(key, shape, cuts, -0.22, 0.18) if cuts else 1.0
    array = jax.random.normal(key, shape, jnp.float32) * deviation * factor_of
    return jnp.minimum(jnp.maximum(array, -bound), bound).astype(kind)


def setup_inputs(seed: int = 0) -> dict:
    streams_of = jax.random.split(jax.random.key(seed), 8)
    start_basis = centred(streams_of[0], (ROWS, K), 1.0, 6.0, ((0, 128),), jnp.float32)
    affinity_tiles = centred(streams_of[1], (DEVICES * NT, BLK, BLK), (BLK * NT * BLK // PIECE) ** -0.5, 0.046875, ((0, 128),))
    tile_rows = draw_tile_rows(jax.random.fold_in(streams_of[7], 71), 0)
    tile_cols = draw_tile_cols(jax.random.fold_in(streams_of[7], 71), 0)
    live_tiles = draw_live_tiles(jax.random.fold_in(streams_of[7], 71), 0)
    filter_center = jnp.clip(jax.random.uniform(streams_of[5], (1,), jnp.float32, -0.3, 0.3), -0.3, 0.3)
    filter_radius = jnp.clip(jax.random.uniform(streams_of[6], (1,), jnp.float32, 0.6, 1.2), 0.6, 1.2)
    return {"start_basis": start_basis, "affinity_tiles": affinity_tiles, "tile_rows": tile_rows, "tile_cols": tile_cols, "live_tiles": live_tiles, "filter_center": filter_center, "filter_radius": filter_radius}


def product(field, affinity_tiles, tile_rows, tile_cols, live_tiles):
    row_span = N_ROW * PIECE_TILES
    col_span = N_COL * PIECE_TILES

    def one_device(device, total):
        device = jnp.asarray(device).astype(jnp.int32)
        row_index = device // N_COL
        col_index = device % N_COL
        column_rows = lax.dynamic_slice_in_dim(field, row_index * (N_COL * PIECE), N_COL * PIECE, 0)
        blocks = column_rows.reshape(col_span, BLK, K)
        slot_tiles = lax.dynamic_slice_in_dim(affinity_tiles, device * NT, NT, 0).astype(jnp.float32)
        slot_rows = lax.dynamic_slice_in_dim(tile_rows, device * NT, NT, 0)
        slot_cols = lax.dynamic_slice_in_dim(tile_cols, device * NT, NT, 0)
        selected = jnp.take(blocks, slot_cols, axis=0)
        products = jnp.einsum('kab,kbj->kaj', slot_tiles, selected, precision=lax.Precision.HIGHEST)
        live_mask = jnp.arange(NT, dtype=jnp.int32) < live_tiles[device]
        row_select = ((slot_rows[None, :] == jnp.arange(row_span, dtype=jnp.int32)[:, None]) & live_mask[None, :]).astype(jnp.float32)
        partial_value = jnp.einsum('ik,kaj->iaj', row_select, products, precision=lax.Precision.HIGHEST)
        partial_value = partial_value.reshape(N_ROW, 1, PIECE, K)
        anchor = jnp.zeros((), jnp.int32)
        starts = (anchor, col_index, anchor, anchor)
        current = lax.dynamic_slice(total, starts, (N_ROW, 1, PIECE, K))
        return lax.dynamic_update_slice(total, current + partial_value, starts)

    total = lax.fori_loop(0, DEVICES, one_device, jnp.zeros((N_ROW, N_COL, PIECE, K), jnp.float32))
    return total.reshape(ROWS, K)


def reference(start_basis, affinity_tiles, tile_rows, tile_cols, live_tiles, filter_center, filter_radius):
    center = filter_center[0]
    radius = filter_radius[0]
    first = (product(start_basis, affinity_tiles, tile_rows, tile_cols, live_tiles) - center * start_basis) / radius
    second = product(first, affinity_tiles, tile_rows, tile_cols, live_tiles)
    return 2.0 * (second - center * first) / radius - start_basis
```

```python
import functools

import jax
import jax.numpy as jnp
from jax import lax
from jax.experimental import pallas as pl
from jax.experimental.pallas import tpu as pltpu
from jax.sharding import PartitionSpec as P

MESH = pl.DeviceIdType.MESH
F32 = jnp.float32
BF16 = jnp.bfloat16
BLK = 256
NT = 144
PIECE = 512
K = 256
NCH = 4
QC = K // NCH
HC = QC // 2
STAGES = 2 * NCH
GROUPS = 80
UNROLL = 16
PARTS = 8
SLOTS = 4


def filter_kernel(
    x_ref, t_hbm, rows_ref, cols_ref, live_ref, cen_ref, rad_ref, o_ref,
    tiles, gath, vals, sums, part, got_a, got_n, got_x, x_t, o_t, ivec, idx,
    t_sem, i_sem, g_send, g_recv, r_send, r_recv,
):
    row = lax.axis_index("row")
    col = lax.axis_index("col")
    xl, z = row // 4, row % 4
    xh, y, core = col // 8, (col // 2) % 4, col % 2

    def dev(xh_, xl_, y_, z_, core_):
        return (xl_ * 4 + z_, xh_ * 8 + y_ * 2 + core_)

    up, down = dev(xh, xl, (y + 1) % 4, z, core), dev(xh, xl, (y + 3) % 4, z, core)
    zup, zdown = dev(xh, xl, y, (z + 1) % 4, core), dev(xh, xl, y, (z + 3) % 4, core)
    sib = dev(xh, xl, y, z, 1 - core)
    far = dev(1 - xh, xl, y, z, core)
    near = dev(xh, 1 - xl, y, z, core)

    per = NT // PARTS

    def tile_copy(i):
        span = pl.ds(i * per, per)
        return pltpu.make_async_copy(t_hbm.at[span], tiles.at[span], t_sem.at[i])

    for i in range(PARTS):
        tile_copy(i).start()

    def send(src, dst, ssem, rsem, to):
        pltpu.make_async_remote_copy(
            src_ref=src, dst_ref=dst, send_sem=ssem, recv_sem=rsem, device_id=to, device_id_type=MESH
        ).start()

    def wait_recv(ref, sem):
        pltpu.make_async_remote_copy(
            src_ref=ref, dst_ref=ref, send_sem=g_send, recv_sem=sem, device_id=sib, device_id_type=MESH
        ).wait_recv()

    def wait_send(ref, sem):
        pltpu.make_async_remote_copy(
            src_ref=ref, dst_ref=ref, send_sem=sem, recv_sem=g_recv.at[0, 0], device_id=sib, device_id_type=MESH
        ).wait_send()

    def piece(k, core_, xh_, y_):
        return gath.at[k * 16 + core_ * 8 + xh_ * 4 + y_]

    lo_half, hi_half = pl.ds(0, HC), pl.ds(HC, HC)
    S_L, S_R, S_X, S_Y2, S_XL, S_XR, S_X2, S_SIB = range(8)

    def to_sib(k, ref):
        send(ref, ref, g_send, g_recv.at[k, S_SIB], sib)

    def gather_own(k):
        own = piece(k, core, xh, y)
        send(own, own, g_send, g_recv.at[k, S_L], up)
        send(own, own, g_send, g_recv.at[k, S_R], down)
        send(own, own, g_send, g_recv.at[k, S_X], far)
        to_sib(k, own)

    def gather_one(k):
        left, right = piece(k, core, xh, (y + 3) % 4), piece(k, core, xh, (y + 1) % 4)
        opp = piece(k, core, 1 - xh, y)
        wait_recv(opp, g_recv.at[k, S_X])
        send(opp, opp, g_send, g_recv.at[k, S_XL], up)
        send(opp, opp, g_send, g_recv.at[k, S_XR], down)
        wait_recv(left, g_recv.at[k, S_L])
        send(left.at[lo_half], left.at[lo_half], g_send, g_recv.at[k, S_Y2], up)
        wait_recv(right, g_recv.at[k, S_R])
        send(right.at[hi_half], right.at[hi_half], g_send, g_recv.at[k, S_Y2], down)
        to_sib(k, opp)
        to_sib(k, left)
        to_sib(k, right)

    def gather_two(k):
        left, right = piece(k, core, 1 - xh, (y + 3) % 4), piece(k, core, 1 - xh, (y + 1) % 4)
        wait_recv(left, g_recv.at[k, S_XL])
        send(left.at[lo_half], left.at[lo_half], g_send, g_recv.at[k, S_X2], up)
        wait_recv(right, g_recv.at[k, S_XR])
        send(right.at[hi_half], right.at[hi_half], g_send, g_recv.at[k, S_X2], down)
        to_sib(k, left)
        to_sib(k, right)

    def gather_end(k):
        mine, other = piece(k, core, xh, (y + 2) % 4), piece(k, core, 1 - xh, (y + 2) % 4)
        wait_recv(mine, g_recv.at[k, S_Y2])
        to_sib(k, mine)
        wait_recv(other, g_recv.at[k, S_X2])
        to_sib(k, other)
        wait_recv(gath.at[pl.ds(k * 16 + (1 - core) * 8, 8)], g_recv.at[k, S_SIB])
        for core_ in range(2):
            for m in range(8):
                block = gath[k * 16 + core_ * 8 + m]
                high = block.astype(BF16)
                low = (block - high.astype(F32)).astype(BF16)
                for t in range(2):
                    j = (2 * m + core_) * 2 + t
                    vals[j, 0:QC] = high[:, t * BLK : (t + 1) * BLK]
                    vals[j, QC : 2 * QC] = low[:, t * BLK : (t + 1) * BLK]

    R_A, R_N, R_X = 0, 2, 4
    sides = (1 - xl, xl)

    def part_at(k, xl_, z_):
        return part.at[(k % SLOTS) * 8 + xl_ * 4 + z_]

    def multiply(k):
        @pl.loop(0, GROUPS // UNROLL)
        def _(i):
            for u in range(UNROLL):
                g = i * UNROLL + u
                p0, p1 = idx[0, 2 * g], idx[0, 2 * g + 1]
                c0, c1 = idx[1, 2 * g], idx[1, 2 * g + 1]
                d = jnp.dot(vals[c0], tiles[p0], preferred_element_type=F32) + jnp.dot(
                    vals[c1], tiles[p1], preferred_element_type=F32
                )
                keep = idx[2, g].astype(F32)
                sums[g + 1] = sums[g] * keep + (d[:QC] + d[QC:])

        @pl.when(k >= SLOTS)
        def _():
            wait_send(part.at[pl.ds(0, 7)], r_send.at[k % SLOTS])

        for i in range(16):
            part[(k % SLOTS) * 8 + i // 2, :, (i % 2) * BLK : (i % 2 + 1) * BLK] = sums[idx[3, i]]
        ssem = r_send.at[k % SLOTS]
        for g in range(2):
            a = part_at(k, sides[g], (z + 2) % 4)
            send(a.at[lo_half], got_a.at[k * 4 + g * 2 + 0], ssem, r_recv.at[k, R_A + g], zup)
            send(a.at[hi_half], got_a.at[k * 4 + g * 2 + 1], ssem, r_recv.at[k, R_A + g], zdown)
        send_plain(k, 0)

    def send_plain(k, g):
        ssem = r_send.at[k % SLOTS]
        n_up, n_down = part_at(k, sides[g], (z + 1) % 4), part_at(k, sides[g], (z + 3) % 4)
        send(n_up.at[hi_half], got_n.at[k * 4 + g * 2 + 0, hi_half], ssem, r_recv.at[k, R_N + g], zup)
        send(n_down.at[lo_half], got_n.at[k * 4 + g * 2 + 1, lo_half], ssem, r_recv.at[k, R_N + g], zdown)

    def reduce_one(k):
        ssem = r_send.at[k % SLOTS]
        for g in range(2):
            wait_recv(got_a.at[pl.ds(k * 4 + g * 2, 2)], r_recv.at[k, R_A + g])
            n_up, n_down = part_at(k, sides[g], (z + 1) % 4), part_at(k, sides[g], (z + 3) % 4)
            n_up[0:HC] = n_up[0:HC] + got_a[k * 4 + g * 2 + 0]
            n_down[HC:QC] = n_down[HC:QC] + got_a[k * 4 + g * 2 + 1]
            send(n_up.at[lo_half], got_n.at[k * 4 + g * 2 + 0, lo_half], ssem, r_recv.at[k, R_N + g], zup)
            send(n_down.at[hi_half], got_n.at[k * 4 + g * 2 + 1, hi_half], ssem, r_recv.at[k, R_N + g], zdown)
            if g == 0:
                send_plain(k, 1)

    def reduce_two(k):
        wait_recv(got_n.at[pl.ds(k * 4, 2)], r_recv.at[k, R_N])
        mine = part_at(k, 1 - xl, z)
        mine[...] = mine[...] + got_n[k * 4] + got_n[k * 4 + 1]
        send(mine, got_x.at[k], r_send.at[k % SLOTS], r_recv.at[k, R_X], near)

    def reduce_end(k):
        wait_recv(got_n.at[pl.ds(k * 4 + 2, 2)], r_recv.at[k, R_N + 1])
        wait_recv(got_x.at[k], r_recv.at[k, R_X])
        mine = part_at(k, xl, z)
        total = mine[...] + got_n[k * 4 + 2] + got_n[k * 4 + 3] + got_x[k]
        center, radius = cen_ref[0], rad_ref[0]
        cols_at = pl.ds(pl.multiple_of((k % NCH) * QC, QC), QC)
        start = x_t[cols_at]

        @pl.when(k < NCH)
        def _():
            gath[(k + NCH) * 16 + core * 8 + xh * 4 + y] = (total - center * start) / radius

        @pl.when(k >= NCH)
        def _():
            first = gath[k * 16 + core * 8 + xh * 4 + y]
            o_t[cols_at] = 2.0 * (total - center * first) / radius - start

    x_t[...] = x_ref[...].T
    for j in range(NCH):
        gath[j * 16 + core * 8 + xh * 4 + y] = x_t[j * QC : (j + 1) * QC]

    barrier = pltpu.get_barrier_semaphore()
    others = (up, down, zup, zdown, sib, far, near)
    for other in others:
        pl.semaphore_signal(barrier, inc=1, device_id=other, device_id_type=MESH)
    pl.semaphore_wait(barrier, len(others))

    gather_own(0)

    ivec[...] = jnp.full(ivec.shape, 99, jnp.int32)
    ivec[0:1, 0:NT] = rows_ref[...]
    ivec[1:2, 0:NT] = cols_ref[...]
    lanes = lax.broadcasted_iota(jnp.int32, (1, 256), 1)
    row_of = jnp.where(lanes < live_ref[0], ivec[0:1], 99)
    row_l = jnp.broadcast_to(row_of, (256, 256))
    row_s = row_l.T
    col_s = jnp.broadcast_to(ivec[1:2], (256, 256)).T
    li = lax.broadcasted_iota(jnp.int32, (256, 256), 1)
    si = lax.broadcasted_iota(jnp.int32, (256, 256), 0)

    def count(mask, value=1, axis=1):
        return jnp.sum(jnp.where(mask, value, 0), axis=axis, keepdims=True)

    within = count((row_l == row_s) & (li < si))
    pairs = (count(row_s == li, axis=0) + 1) >> 1
    before = count(li < row_s, pairs)
    pairs_s = count(li == row_s, pairs)
    live = row_s < 16
    place = live & (2 * before + within == li)
    leads = live & (within == 0)
    ivec[0:1] = count(place, si, 0)
    ivec[1:2] = count(place, col_s - 32, 0) + 32
    ivec[2:3] = 1 - count(leads & (before == li), 1, 0)
    ivec[3:4] = count(leads & (row_s <= li), pairs_s, 0)
    to_smem = pltpu.make_async_copy(ivec, idx, i_sem)
    to_smem.start()

    def turn(i):
        tile_copy(i).wait()

        @pl.loop(0, per)
        def _(s):
            tiles[i * per + s] = tiles[i * per + s].T

    vals[32] = jnp.zeros((2 * QC, BLK), BF16)
    sums[0] = jnp.zeros((QC, BLK), F32)
    for i in range(PARTS // 2):
        turn(i)
    gather_one(0)
    gather_own(1)
    for i in range(PARTS // 2, PARTS):
        turn(i)
    gather_two(0)
    to_smem.wait()

    @pl.loop(1, STAGES + 3)
    def _(k):
        @pl.when(k <= STAGES)
        def _():
            gather_end(k - 1)

        @pl.when(k >= 3)
        def _():
            reduce_end(k - 3)

        @pl.when((k >= 2) & (k < STAGES + 2))
        def _():
            reduce_one(k - 2)

        @pl.when(k < STAGES)
        def _():
            gather_one(k)

        @pl.when(k < STAGES - 1)
        def _():
            gather_own(k + 1)

        @pl.when(k <= STAGES)
        def _():
            multiply(k - 1)

        @pl.when(k < STAGES)
        def _():
            gather_two(k)

        @pl.when((k >= 2) & (k < STAGES + 2))
        def _():
            reduce_two(k - 2)

    wait_send(gath.at[pl.ds(0, 15 * STAGES)], g_send)
    for s in range(SLOTS):
        wait_send(part.at[pl.ds(0, 7)], r_send.at[s])
    o_ref[...] = o_t[...].T


def local(start_basis, affinity_tiles, tile_rows, tile_cols, live_tiles, filter_center, filter_radius):
    vmem = pl.BlockSpec(memory_space=pltpu.VMEM)
    smem = pl.BlockSpec(memory_space=pltpu.SMEM)
    return pl.pallas_call(
        filter_kernel,
        name="chebyshev_filter",
        out_shape=jax.ShapeDtypeStruct((PIECE, K), F32),
        in_specs=[vmem, pl.BlockSpec(memory_space=pl.ANY), vmem, vmem, smem, smem, smem],
        out_specs=vmem,
        scratch_shapes=[
            pltpu.VMEM((NT, BLK, BLK), BF16),
            pltpu.VMEM((STAGES * 16, QC, PIECE), F32),
            pltpu.VMEM((33, 2 * QC, BLK), BF16),
            pltpu.VMEM((GROUPS + 1, QC, BLK), F32),
            pltpu.VMEM((SLOTS * 8, QC, PIECE), F32),
            pltpu.VMEM((STAGES * 4, HC, PIECE), F32),
            pltpu.VMEM((STAGES * 4, QC, PIECE), F32),
            pltpu.VMEM((STAGES, QC, PIECE), F32),
            pltpu.VMEM((K, PIECE), F32),
            pltpu.VMEM((K, PIECE), F32),
            pltpu.VMEM((8, 256), jnp.int32),
            pltpu.SMEM((8, 256), jnp.int32),
            pltpu.SemaphoreType.DMA((PARTS,)),
            pltpu.SemaphoreType.DMA,
            pltpu.SemaphoreType.DMA,
            pltpu.SemaphoreType.DMA((STAGES, 8)),
            pltpu.SemaphoreType.DMA((SLOTS,)),
            pltpu.SemaphoreType.DMA((STAGES, 5)),
        ],
        compiler_params=pltpu.CompilerParams(
            collective_id=0, has_side_effects=True, vmem_limit_bytes=60 * 2**20
        ),
        cost_estimate=pl.CostEstimate(
            flops=4 * NT * BLK * BLK * K * 2, bytes_accessed=NT * BLK * BLK * 2, transcendentals=0
        ),
    )(
        start_basis, affinity_tiles, tile_rows.reshape(1, NT), tile_cols.reshape(1, NT),
        live_tiles, filter_center, filter_radius,
    )


def solution(mesh):
    return jax.shard_map(
        local,
        mesh=mesh,
        in_specs=(
            P(("row", "col"), None),
            P(("row", "col"), None, None),
            P(("row", "col")),
            P(("row", "col")),
            P(("row", "col")),
            P(),
            P(),
        ),
        out_specs=P(("row", "col"), None),
        check_vma=False,
    )
```

```python
import functools

import jax
import jax.numpy as jnp
from jax import lax
from jax.experimental import pallas as pl
from jax.experimental.pallas import tpu as pltpu
from jax.sharding import PartitionSpec as P

MESH = pl.DeviceIdType.MESH
F32 = jnp.float32
BF16 = jnp.bfloat16
BLK = 256
NT = 144
PIECE = 512
K = 256
CHUNKS = (64, 64, 64, 64)
NCH = len(CHUNKS)
STAGES = 2 * NCH
Q = CHUNKS + CHUNKS
QMAX = max(CHUNKS)
OFF = tuple(sum(Q[:k]) for k in range(STAGES))
GROUPS = 80
UNROLL = 16
PARTS = 8
SLOTS = 4
BY_X = (0, 1, 2, 3)
DIRECT = ()
CORNER = ()
X_FIRST = (6, 7)
ORDER = (
    ("turn", 0), ("turn", 1), ("turn", 2), ("ring", 0), ("turn", 3), ("far", 0), ("ring", 1), ("turn", 4),
    ("last", 0), ("turn", 5), ("own", 2), ("turn", 6), ("far", 1), ("far_ring", 0), ("far_last", 0),
    ("last", 1), ("own", 3), ("turn", 7), ("ring", 2), ("split", 0), ("mul", 0, 0, 2), ("far_ring", 1),
    ("mul", 0, 2, 4), ("far_last", 1), ("far", 2), ("mul", 0, 4, 5), ("start", 0), ("last", 2), ("split", 1),
    ("ring", 3), ("mul", 1, 0, 2), ("pass0", 0), ("far_ring", 2), ("mul", 1, 2, 3), ("last", 3), ("pass1", 0),
    ("mul", 1, 3, 4), ("far_last", 2), ("mul", 1, 4, 5), ("start", 1), ("cross", 0), ("far", 3), ("split", 2),
    ("mul", 2, 0, 3), ("pass0", 1), ("end", 0), ("own", 4), ("far_ring", 3), ("pass1", 1), ("mul", 2, 3, 4),
    ("far_last", 3), ("mul", 2, 4, 5), ("start", 2), ("cross", 1), ("split", 3), ("ring", 4),
    ("mul", 3, 0, 1), ("far", 4), ("mul", 3, 1, 3), ("pass0", 2), ("end", 1), ("pass1", 2), ("own", 5),
    ("mul", 3, 3, 5), ("start", 3), ("far_ring", 4), ("cross", 2), ("ring", 5), ("far", 5), ("last", 4),
    ("far_last", 4), ("pass0", 3), ("end", 2), ("own", 6), ("split", 4), ("mul", 4, 0, 1), ("pass1", 3),
    ("mul", 4, 1, 2), ("far_ring", 5), ("cross", 3), ("last", 5), ("mul", 4, 2, 4), ("far", 6),
    ("mul", 4, 4, 5), ("start", 4), ("far_last", 5), ("ring", 6), ("end", 3), ("own", 7), ("split", 5),
    ("mul", 5, 0, 1), ("far_ring", 6), ("mul", 5, 1, 2), ("last", 6), ("mul", 5, 2, 3), ("pass0", 4),
    ("mul", 5, 3, 4), ("far", 7), ("mul", 5, 4, 5), ("start", 5), ("far_last", 6), ("pass1", 4), ("ring", 7),
    ("cross", 4), ("split", 6), ("far_ring", 7), ("pass0", 5), ("mul", 6, 0, 2), ("pass1", 5), ("last", 7),
    ("mul", 6, 2, 3), ("far_last", 7), ("mul", 6, 3, 5), ("start", 6), ("split", 7), ("mul", 7, 0, 5),
    ("start", 7), ("first", 6), ("cross", 5), ("cross", 6), ("end", 4), ("cross", 7), ("first", 7),
    ("end", 5), ("pass1", 6), ("pass1", 7), ("end", 6), ("end", 7),
)


def filter_kernel(
    x_ref, t_hbm, rows_ref, cols_ref, live_ref, cen_ref, rad_ref, o_ref,
    tiles, gath, vals, sums, part, got_a, got_n, got_x, got_f, x_v, x_t, o_t, ivec, idx,
    x_sem, t_sem, i_sem, g_send, g_recv, r_send, r_recv,
):
    row = lax.axis_index("row")
    col = lax.axis_index("col")
    xl, z = row // 4, row % 4
    xh, y, core = col // 8, (col // 2) % 4, col % 2

    def dev(xh_, xl_, y_, z_, core_):
        return (xl_ * 4 + z_, xh_ * 8 + y_ * 2 + core_)

    up, down = dev(xh, xl, (y + 1) % 4, z, core), dev(xh, xl, (y + 3) % 4, z, core)
    zup, zdown = dev(xh, xl, y, (z + 1) % 4, core), dev(xh, xl, y, (z + 3) % 4, core)
    sib = dev(xh, xl, y, z, 1 - core)
    far = dev(1 - xh, xl, y, z, core)
    near = dev(xh, 1 - xl, y, z, core)
    corner_up, corner_down = dev(xh, 1 - xl, y, (z + 1) % 4, core), dev(xh, 1 - xl, y, (z + 3) % 4, core)
    opposite, far_opposite = dev(xh, xl, (y + 2) % 4, z, core), dev(1 - xh, xl, (y + 2) % 4, z, core)
    far_up, far_down = dev(1 - xh, xl, (y + 1) % 4, z, core), dev(1 - xh, xl, (y + 3) % 4, z, core)

    x_copy = pltpu.make_async_copy(x_ref, x_v, x_sem)
    x_copy.start()
    barrier = pltpu.get_barrier_semaphore()
    others = (up, down, zup, zdown, sib, far, near)
    if CORNER:
        others += (corner_up, corner_down)
    if DIRECT:
        others += (opposite, far_opposite, far_up, far_down)
    for other in others:
        pl.semaphore_signal(barrier, inc=1, device_id=other, device_id_type=MESH)

    per = NT // PARTS

    def tile_copy(i):
        span = pl.ds(i * per, per)
        return pltpu.make_async_copy(t_hbm.at[span], tiles.at[span], t_sem.at[i])

    for i in range(PARTS):
        tile_copy(i).start()

    def send(src, dst, ssem, rsem, to):
        pltpu.make_async_remote_copy(
            src_ref=src, dst_ref=dst, send_sem=ssem, recv_sem=rsem, device_id=to, device_id_type=MESH
        ).start()

    def wait_recv(ref, sem):
        pltpu.make_async_remote_copy(
            src_ref=ref, dst_ref=ref, send_sem=g_send, recv_sem=sem, device_id=sib, device_id_type=MESH
        ).wait_recv()

    def wait_send(ref, sem):
        pltpu.make_async_remote_copy(
            src_ref=ref, dst_ref=ref, send_sem=sem, recv_sem=g_recv.at[0, 0], device_id=sib, device_id_type=MESH
        ).wait_send()

    def rows(ref, start, count):
        return ref.at[pl.ds(start if isinstance(start, int) else pl.multiple_of(start, 16), count)]

    def piece(k, core_, xh_, y_):
        return rows(gath, 16 * OFF[k] + (core_ * 8 + xh_ * 4 + y_) * Q[k], Q[k])

    def halves(k):
        return pl.ds(0, Q[k] // 2), pl.ds(Q[k] // 2, Q[k] // 2)

    S_L, S_R, S_X, S_Y2, S_XL, S_XR, S_X2, S_SIB = range(8)

    def to_sib(k, ref):
        send(ref, ref, g_send, g_recv.at[k, S_SIB], sib)

    def gather_own(k):
        own = piece(k, core, xh, y)
        send(own, own, g_send, g_recv.at[k, S_L], up)
        send(own, own, g_send, g_recv.at[k, S_R], down)
        send(own, own, g_send, g_recv.at[k, S_X], far)
        to_sib(k, own)
        if k in DIRECT:
            send(own, own, g_send, g_recv.at[k, S_Y2], opposite)
            send(own, own, g_send, g_recv.at[k, S_XL], far_up)
            send(own, own, g_send, g_recv.at[k, S_XR], far_down)
            send(own, own, g_send, g_recv.at[k, S_X2], far_opposite)

    def gather_far(k):
        opp = piece(k, core, 1 - xh, y)
        wait_recv(opp, g_recv.at[k, S_X])
        if k not in DIRECT:
            send(opp, opp, g_send, g_recv.at[k, S_XL], up)
            send(opp, opp, g_send, g_recv.at[k, S_XR], down)
        to_sib(k, opp)

    def gather_ring(k):
        left, right = piece(k, core, xh, (y + 3) % 4), piece(k, core, xh, (y + 1) % 4)
        lo_half, hi_half = halves(k)
        wait_recv(left, g_recv.at[k, S_L])
        if k not in DIRECT:
            send(left.at[lo_half], left.at[lo_half], g_send, g_recv.at[k, S_Y2], up)
        wait_recv(right, g_recv.at[k, S_R])
        if k not in DIRECT:
            send(right.at[hi_half], right.at[hi_half], g_send, g_recv.at[k, S_Y2], down)
        to_sib(k, left)
        to_sib(k, right)

    def gather_far_ring(k):
        left, right = piece(k, core, 1 - xh, (y + 3) % 4), piece(k, core, 1 - xh, (y + 1) % 4)
        lo_half, hi_half = halves(k)
        wait_recv(left, g_recv.at[k, S_XL])
        wait_recv(right, g_recv.at[k, S_XR])
        if k not in BY_X and k not in DIRECT:
            send(left.at[lo_half], left.at[lo_half], g_send, g_recv.at[k, S_X2], up)
            send(right.at[hi_half], right.at[hi_half], g_send, g_recv.at[k, S_X2], down)
        to_sib(k, left)
        to_sib(k, right)

    def gather_last(k):
        mine = piece(k, core, xh, (y + 2) % 4)
        wait_recv(mine, g_recv.at[k, S_Y2])
        to_sib(k, mine)
        if k in BY_X:
            send(mine, mine, g_send, g_recv.at[k, S_X2], far)

    def gather_far_last(k):
        other = piece(k, core, 1 - xh, (y + 2) % 4)
        wait_recv(other, g_recv.at[k, S_X2])
        to_sib(k, other)

    def split(k):
        q = Q[k]
        wait_recv(rows(gath, 16 * OFF[k] + (1 - core) * 8 * q, 8 * q), g_recv.at[k, S_SIB])
        for core_ in range(2):
            for m in range(8):
                block = rows(gath, 16 * OFF[k] + (core_ * 8 + m) * q, q)[...]
                high = block.astype(BF16)
                low = (block - high.astype(F32)).astype(BF16)
                for t in range(2):
                    j = (2 * m + core_) * 2 + t
                    vals[j, 0:q] = high[:, t * BLK : (t + 1) * BLK]
                    vals[j, q : 2 * q] = low[:, t * BLK : (t + 1) * BLK]

    R_A, R_N, R_X = 0, 2, 4
    sides = (1 - xl, xl)

    def part_at(k, xl_, z_):
        return rows(part, (k % SLOTS) * 8 * QMAX + (xl_ * 4 + z_) * Q[k], Q[k])

    def got_a_at(k, g, side, count=1):
        return rows(got_a, 2 * OFF[k] + (g * 2 + side) * (Q[k] // 2), count * (Q[k] // 2))

    def got_n_at(k, g, side, count=1):
        return rows(got_n, 4 * OFF[k] + (g * 2 + side) * Q[k], count * Q[k])

    def multiply(k, lo, hi):
        q = Q[k]

        @pl.loop(lo, hi)
        def _(i):
            for u in range(UNROLL):
                g = i * UNROLL + u
                p0, p1 = idx[0, 2 * g], idx[0, 2 * g + 1]
                c0, c1 = idx[1, 2 * g], idx[1, 2 * g + 1]
                d = jnp.dot(vals[c0, 0 : 2 * q], tiles[p0], preferred_element_type=F32) + jnp.dot(
                    vals[c1, 0 : 2 * q], tiles[p1], preferred_element_type=F32
                )
                keep = idx[2, g].astype(F32)
                sums[g + 1, 0:q] = sums[g, 0:q] * keep + (d[:q] + d[q:])

    def send_n(k, g, half_up, half_down):
        ssem = r_send.at[k % SLOTS]
        n_up, n_down = part_at(k, sides[g], (z + 1) % 4), part_at(k, sides[g], (z + 3) % 4)
        to_up, to_down = (corner_up, corner_down) if k in CORNER and g == 0 else (zup, zdown)
        send(n_up.at[half_up], got_n_at(k, g, 0).at[half_up], ssem, r_recv.at[k, R_N + g], to_up)
        send(n_down.at[half_down], got_n_at(k, g, 1).at[half_down], ssem, r_recv.at[k, R_N + g], to_down)

    def send_a(k, g):
        ssem = r_send.at[k % SLOTS]
        lo_half, hi_half = halves(k)
        a = part_at(k, sides[g], (z + 2) % 4)
        send(a.at[lo_half], got_a_at(k, g, 0), ssem, r_recv.at[k, R_A + g], zup)
        send(a.at[hi_half], got_a_at(k, g, 1), ssem, r_recv.at[k, R_A + g], zdown)

    def reduce_start(k):
        q = Q[k]
        lo_half, hi_half = halves(k)
        if k >= SLOTS:
            wait_send(rows(part, 0, 7 * Q[k - SLOTS]), r_send.at[k % SLOTS])
        base = (k % SLOTS) * 8 * QMAX
        for i in range(16):
            at = base + (i // 2) * q
            part[at : at + q, (i % 2) * BLK : (i % 2 + 1) * BLK] = sums[idx[3, i], 0:q]
        if k in X_FIRST:
            a = part_at(k, 1 - xl, (z + 2) % 4)
            send(a, rows(got_f, OFF[k], q), r_send.at[k % SLOTS], r_recv.at[k, R_A], near)
            send_n(k, 0, pl.ds(0, q), pl.ds(0, q))
        else:
            send_a(k, 0)
            send_a(k, 1)
            send_n(k, 0, hi_half, lo_half)
        if k in CORNER:
            send(part_at(k, 1 - xl, z), rows(got_x, OFF[k], q), r_send.at[k % SLOTS], r_recv.at[k, R_X], near)

    def reduce_first(k):
        lo_half, hi_half = halves(k)
        got = rows(got_f, OFF[k], Q[k])
        wait_recv(got, r_recv.at[k, R_A])
        a = part_at(k, xl, (z + 2) % 4)
        a[...] = a[...] + got[...]
        send_a(k, 1)
        send_n(k, 1, hi_half, lo_half)

    def reduce_pass(k, g):
        h = Q[k] // 2
        lo_half, hi_half = halves(k)
        wait_recv(got_a_at(k, g, 0, 2), r_recv.at[k, R_A + g])
        n_up, n_down = part_at(k, sides[g], (z + 1) % 4), part_at(k, sides[g], (z + 3) % 4)
        n_up[0:h] = n_up[0:h] + got_a_at(k, g, 0)[...]
        n_down[h : 2 * h] = n_down[h : 2 * h] + got_a_at(k, g, 1)[...]
        send_n(k, g, lo_half, hi_half)
        if g == 0:
            send_n(k, 1, hi_half, lo_half)

    def reduce_two(k):
        wait_recv(got_n_at(k, 0, 0, 2), r_recv.at[k, R_N])
        mine = part_at(k, 1 - xl, z)
        mine[...] = mine[...] + got_n_at(k, 0, 0)[...] + got_n_at(k, 0, 1)[...]
        send(mine, rows(got_x, OFF[k], Q[k]), r_send.at[k % SLOTS], r_recv.at[k, R_X], near)

    def reduce_end(k):
        got = rows(got_x, OFF[k], Q[k])
        wait_recv(got_n_at(k, 1, 0, 2), r_recv.at[k, R_N + 1])
        wait_recv(got, r_recv.at[k, R_X])
        mine = part_at(k, xl, z)
        total = mine[...] + got_n_at(k, 1, 0)[...] + got_n_at(k, 1, 1)[...] + got[...]
        if k in CORNER:
            wait_recv(got_n_at(k, 0, 0, 2), r_recv.at[k, R_N])
            total = total + got_n_at(k, 0, 0)[...] + got_n_at(k, 0, 1)[...]
        center, radius = cen_ref[0], rad_ref[0]
        cols_at = pl.ds(OFF[k % NCH], Q[k])
        start = x_t[cols_at]
        if k < NCH:
            piece(k + NCH, core, xh, y)[...] = (total - center * start) / radius
        else:
            first = piece(k, core, xh, y)[...]
            o_t[cols_at] = 2.0 * (total - center * first) / radius - start

    x_copy.wait()
    x_t[...] = x_v[...].T
    for j in range(NCH):
        piece(j, core, xh, y)[...] = x_t[OFF[j] : OFF[j] + Q[j]]
    pl.semaphore_wait(barrier, len(others))

    gather_own(0)
    gather_own(1)

    ivec[...] = jnp.full(ivec.shape, 99, jnp.int32)
    ivec[0:1, 0:NT] = rows_ref[...]
    ivec[1:2, 0:NT] = cols_ref[...]
    lanes = lax.broadcasted_iota(jnp.int32, (1, 256), 1)
    row_of = jnp.where(lanes < live_ref[0], ivec[0:1], 99)
    row_l = jnp.broadcast_to(row_of, (256, 256))
    row_s = row_l.T
    col_s = jnp.broadcast_to(ivec[1:2], (256, 256)).T
    li = lax.broadcasted_iota(jnp.int32, (256, 256), 1)
    si = lax.broadcasted_iota(jnp.int32, (256, 256), 0)

    def count(mask, value=1, axis=1):
        return jnp.sum(jnp.where(mask, value, 0), axis=axis, keepdims=True)

    within = count((row_l == row_s) & (li < si))
    pairs = (count(row_s == li, axis=0) + 1) >> 1
    before = count(li < row_s, pairs)
    pairs_s = count(li == row_s, pairs)
    live = row_s < 16
    place = live & (2 * before + within == li)
    leads = live & (within == 0)
    ivec[0:1] = count(place, si, 0)
    ivec[1:2] = count(place, col_s - 32, 0) + 32
    ivec[2:3] = 1 - count(leads & (before == li), 1, 0)
    ivec[3:4] = count(leads & (row_s <= li), pairs_s, 0)
    to_smem = pltpu.make_async_copy(ivec, idx, i_sem)
    to_smem.start()

    def turn(i):
        tile_copy(i).wait()

        @pl.loop(0, per // 6)
        def _(s):
            for u in range(6):
                at = i * per + s * 6 + u
                tiles[at] = tiles[at].T

    vals[32] = jnp.zeros((2 * QMAX, BLK), BF16)
    sums[0] = jnp.zeros((QMAX, BLK), F32)

    step = {
        "own": gather_own, "far": gather_far, "ring": gather_ring, "far_ring": gather_far_ring,
        "last": gather_last, "far_last": gather_far_last, "split": split, "start": reduce_start,
        "first": reduce_first, "pass0": lambda k: reduce_pass(k, 0), "pass1": lambda k: reduce_pass(k, 1),
        "cross": reduce_two, "end": reduce_end, "turn": turn,
    }
    multiplied = 0
    for name, k, *span in ORDER:
        if name == "mul":
            if multiplied == 0 and k == 0:
                to_smem.wait()
                multiplied = 1
            multiply(k, *span)
        else:
            step[name](k)

    wait_send(rows(gath, 0, 15 * 2 * K), g_send)
    for k in range(STAGES - SLOTS, STAGES):
        wait_send(rows(part, 0, 7 * Q[k]), r_send.at[k % SLOTS])
    o_ref[...] = o_t[...].T


def local(start_basis, affinity_tiles, tile_rows, tile_cols, live_tiles, filter_center, filter_radius):
    vmem = pl.BlockSpec(memory_space=pltpu.VMEM)
    smem = pl.BlockSpec(memory_space=pltpu.SMEM)
    return pl.pallas_call(
        filter_kernel,
        name="chebyshev_filter",
        out_shape=jax.ShapeDtypeStruct((PIECE, K), F32),
        in_specs=[pl.BlockSpec(memory_space=pl.ANY), pl.BlockSpec(memory_space=pl.ANY), vmem, vmem, smem, smem, smem],
        out_specs=vmem,
        scratch_shapes=[
            pltpu.VMEM((NT, BLK, BLK), BF16),
            pltpu.VMEM((16 * 2 * K, PIECE), F32),
            pltpu.VMEM((33, 2 * QMAX, BLK), BF16),
            pltpu.VMEM((GROUPS + 1, QMAX, BLK), F32),
            pltpu.VMEM((SLOTS * 8 * QMAX, PIECE), F32),
            pltpu.VMEM((2 * 2 * K, PIECE), F32),
            pltpu.VMEM((4 * 2 * K, PIECE), F32),
            pltpu.VMEM((2 * K, PIECE), F32),
            pltpu.VMEM((2 * K, PIECE), F32),
            pltpu.VMEM((PIECE, K), F32),
            pltpu.VMEM((K, PIECE), F32),
            pltpu.VMEM((K, PIECE), F32),
            pltpu.VMEM((8, 256), jnp.int32),
            pltpu.SMEM((8, 256), jnp.int32),
            pltpu.SemaphoreType.DMA,
            pltpu.SemaphoreType.DMA((PARTS,)),
            pltpu.SemaphoreType.DMA,
            pltpu.SemaphoreType.DMA,
            pltpu.SemaphoreType.DMA((STAGES, 8)),
            pltpu.SemaphoreType.DMA((SLOTS,)),
            pltpu.SemaphoreType.DMA((STAGES, 5)),
        ],
        compiler_params=pltpu.CompilerParams(
            collective_id=0, has_side_effects=True, vmem_limit_bytes=60 * 2**20
        ),
        cost_estimate=pl.CostEstimate(
            flops=4 * NT * BLK * BLK * K * 2, bytes_accessed=NT * BLK * BLK * 2, transcendentals=0
        ),
    )(
        start_basis, affinity_tiles, tile_rows.reshape(1, NT), tile_cols.reshape(1, NT),
        live_tiles, filter_center, filter_radius,
    )


def solution(mesh):
    return jax.shard_map(
        local,
        mesh=mesh,
        in_specs=(
            P(("row", "col"), None),
            P(("row", "col"), None, None),
            P(("row", "col")),
            P(("row", "col")),
            P(("row", "col")),
            P(),
            P(),
        ),
        out_specs=P(("row", "col"), None),
        check_vma=False,
    )
```

```python
import functools

import jax
import jax.numpy as jnp
from jax import lax
from jax.experimental import pallas as pl
from jax.experimental.pallas import tpu as pltpu
from jax.sharding import PartitionSpec as P

MESH = pl.DeviceIdType.MESH
F32 = jnp.float32
BF16 = jnp.bfloat16
BLK = 256
NT = 144
PIECE = 512
K = 256
CHUNKS = (48, 48, 48, 48, 64)
NCH = len(CHUNKS)
STAGES = 2 * NCH
Q = CHUNKS + CHUNKS
QMAX = max(CHUNKS)
OFF = tuple(sum(Q[:k]) for k in range(STAGES))
GROUPS = 80
UNROLL = 16
PARTS = 8
SLOTS = 4
BY_X = (0, 1, 2, 3, 4)
DIRECT = ()
CORNER = ()
X_FIRST = (8, 9)
ORDER = (
    ("turn", 0), ("turn", 1), ("ring", 0), ("far", 0), ("turn", 2), ("own", 2), ("turn", 3), ("turn", 4),
    ("ring", 1), ("last", 0), ("turn", 5), ("far_ring", 0), ("own", 3), ("far", 1), ("turn", 6), ("turn", 7),
    ("far_last", 0), ("last", 1), ("ring", 2), ("own", 4), ("split", 0), ("mul", 0, 0, 1), ("far", 2),
    ("mul", 0, 1, 2), ("ring", 3), ("far", 3), ("mul", 0, 2, 4), ("far_ring", 1), ("far_last", 1),
    ("last", 2), ("mul", 0, 4, 5), ("start", 0), ("split", 1), ("mul", 1, 0, 3), ("ring", 4), ("far_ring", 2),
    ("far", 4), ("pass0", 0), ("mul", 1, 3, 4), ("last", 3), ("far_last", 2), ("mul", 1, 4, 5), ("start", 1),
    ("split", 2), ("pass1", 0), ("mul", 2, 0, 1), ("cross", 0), ("last", 4), ("mul", 2, 1, 2),
    ("far_ring", 3), ("mul", 2, 2, 3), ("far_last", 3), ("pass0", 1), ("mul", 2, 3, 5), ("start", 2),
    ("split", 3), ("end", 0), ("own", 5), ("mul", 3, 0, 1), ("pass1", 1), ("cross", 1), ("far_ring", 4),
    ("mul", 3, 1, 3), ("pass0", 2), ("mul", 3, 3, 4), ("far_last", 4), ("mul", 3, 4, 5), ("start", 3),
    ("far", 5), ("split", 4), ("mul", 4, 0, 1), ("end", 1), ("own", 6), ("cross", 2), ("pass1", 2),
    ("ring", 5), ("mul", 4, 1, 3), ("pass0", 3), ("mul", 4, 3, 4), ("far_ring", 5), ("pass1", 3),
    ("mul", 4, 4, 5), ("start", 4), ("far", 6), ("last", 5), ("cross", 3), ("ring", 6), ("far_last", 5),
    ("end", 2), ("own", 7), ("split", 5), ("mul", 5, 0, 1), ("pass0", 4), ("far_ring", 6), ("mul", 5, 1, 2),
    ("end", 3), ("own", 8), ("mul", 5, 2, 3), ("last", 6), ("mul", 5, 3, 4), ("far", 7), ("cross", 4),
    ("far_last", 6), ("ring", 7), ("pass1", 4), ("mul", 5, 4, 5), ("start", 5), ("split", 6), ("far", 8),
    ("mul", 6, 0, 2), ("far_ring", 7), ("mul", 6, 2, 3), ("end", 4), ("own", 9), ("pass0", 5), ("last", 7),
    ("mul", 6, 3, 4), ("far_ring", 8), ("ring", 8), ("pass1", 5), ("far_last", 7), ("mul", 6, 4, 5),
    ("start", 6), ("split", 7), ("cross", 5), ("mul", 7, 0, 1), ("far", 9), ("mul", 7, 1, 3), ("far_last", 8),
    ("last", 8), ("pass0", 6), ("mul", 7, 3, 4), ("ring", 9), ("mul", 7, 4, 5), ("start", 7), ("pass1", 6),
    ("end", 5), ("split", 8), ("far_ring", 9), ("mul", 8, 0, 4), ("last", 9), ("pass0", 7), ("cross", 6),
    ("pass1", 7), ("far_last", 9), ("mul", 8, 4, 5), ("start", 8), ("split", 9), ("mul", 9, 0, 5),
    ("start", 9), ("first", 8), ("cross", 7), ("first", 9), ("cross", 8), ("cross", 9), ("end", 7),
    ("pass1", 8), ("pass1", 9), ("end", 8), ("end", 6), ("end", 9),
)


def filter_kernel(
    x_ref, t_hbm, rows_ref, cols_ref, live_ref, cen_ref, rad_ref, o_ref,
    tiles, gath, vals, sums, part, got_a, got_n, got_x, got_f, x_v, x_t, o_t, ivec, idx,
    x_sem, t_sem, i_sem, g_send, g_recv, r_send, r_recv,
):
    row = lax.axis_index("row")
    col = lax.axis_index("col")
    xl, z = row // 4, row % 4
    xh, y, core = col // 8, (col // 2) % 4, col % 2

    def dev(xh_, xl_, y_, z_, core_):
        return (xl_ * 4 + z_, xh_ * 8 + y_ * 2 + core_)

    up, down = dev(xh, xl, (y + 1) % 4, z, core), dev(xh, xl, (y + 3) % 4, z, core)
    zup, zdown = dev(xh, xl, y, (z + 1) % 4, core), dev(xh, xl, y, (z + 3) % 4, core)
    sib = dev(xh, xl, y, z, 1 - core)
    far = dev(1 - xh, xl, y, z, core)
    near = dev(xh, 1 - xl, y, z, core)
    corner_up, corner_down = dev(xh, 1 - xl, y, (z + 1) % 4, core), dev(xh, 1 - xl, y, (z + 3) % 4, core)
    opposite, far_opposite = dev(xh, xl, (y + 2) % 4, z, core), dev(1 - xh, xl, (y + 2) % 4, z, core)
    far_up, far_down = dev(1 - xh, xl, (y + 1) % 4, z, core), dev(1 - xh, xl, (y + 3) % 4, z, core)

    x_copy = pltpu.make_async_copy(x_ref, x_v, x_sem)
    x_copy.start()
    barrier = pltpu.get_barrier_semaphore()
    others = (up, down, zup, zdown, sib, far, near)
    if CORNER:
        others += (corner_up, corner_down)
    if DIRECT:
        others += (opposite, far_opposite, far_up, far_down)
    for other in others:
        pl.semaphore_signal(barrier, inc=1, device_id=other, device_id_type=MESH)

    per = NT // PARTS

    def tile_copy(i):
        span = pl.ds(i * per, per)
        return pltpu.make_async_copy(t_hbm.at[span], tiles.at[span], t_sem.at[i])

    for i in range(PARTS):
        tile_copy(i).start()

    def send(src, dst, ssem, rsem, to):
        pltpu.make_async_remote_copy(
            src_ref=src, dst_ref=dst, send_sem=ssem, recv_sem=rsem, device_id=to, device_id_type=MESH
        ).start()

    def wait_recv(ref, sem):
        pltpu.make_async_remote_copy(
            src_ref=ref, dst_ref=ref, send_sem=g_send, recv_sem=sem, device_id=sib, device_id_type=MESH
        ).wait_recv()

    def wait_send(ref, sem):
        pltpu.make_async_remote_copy(
            src_ref=ref, dst_ref=ref, send_sem=sem, recv_sem=g_recv.at[0, 0], device_id=sib, device_id_type=MESH
        ).wait_send()

    def rows(ref, start, count):
        return ref.at[pl.ds(start if isinstance(start, int) else pl.multiple_of(start, 16), count)]

    def piece(k, core_, xh_, y_):
        return rows(gath, 16 * OFF[k] + (core_ * 8 + xh_ * 4 + y_) * Q[k], Q[k])

    def halves(k):
        return pl.ds(0, Q[k] // 2), pl.ds(Q[k] // 2, Q[k] // 2)

    S_L, S_R, S_X, S_Y2, S_XL, S_XR, S_X2, S_SIB = range(8)

    def to_sib(k, ref):
        send(ref, ref, g_send, g_recv.at[k, S_SIB], sib)

    def gather_own(k):
        own = piece(k, core, xh, y)
        send(own, own, g_send, g_recv.at[k, S_L], up)
        send(own, own, g_send, g_recv.at[k, S_R], down)
        send(own, own, g_send, g_recv.at[k, S_X], far)
        to_sib(k, own)
        if k in DIRECT:
            send(own, own, g_send, g_recv.at[k, S_Y2], opposite)
            send(own, own, g_send, g_recv.at[k, S_XL], far_up)
            send(own, own, g_send, g_recv.at[k, S_XR], far_down)
            send(own, own, g_send, g_recv.at[k, S_X2], far_opposite)

    def gather_far(k):
        opp = piece(k, core, 1 - xh, y)
        wait_recv(opp, g_recv.at[k, S_X])
        if k not in DIRECT:
            send(opp, opp, g_send, g_recv.at[k, S_XL], up)
            send(opp, opp, g_send, g_recv.at[k, S_XR], down)
        to_sib(k, opp)

    def gather_ring(k):
        left, right = piece(k, core, xh, (y + 3) % 4), piece(k, core, xh, (y + 1) % 4)
        lo_half, hi_half = halves(k)
        wait_recv(left, g_recv.at[k, S_L])
        if k not in DIRECT:
            send(left.at[lo_half], left.at[lo_half], g_send, g_recv.at[k, S_Y2], up)
        wait_recv(right, g_recv.at[k, S_R])
        if k not in DIRECT:
            send(right.at[hi_half], right.at[hi_half], g_send, g_recv.at[k, S_Y2], down)
        to_sib(k, left)
        to_sib(k, right)

    def gather_far_ring(k):
        left, right = piece(k, core, 1 - xh, (y + 3) % 4), piece(k, core, 1 - xh, (y + 1) % 4)
        lo_half, hi_half = halves(k)
        wait_recv(left, g_recv.at[k, S_XL])
        wait_recv(right, g_recv.at[k, S_XR])
        if k not in BY_X and k not in DIRECT:
            send(left.at[lo_half], left.at[lo_half], g_send, g_recv.at[k, S_X2], up)
            send(right.at[hi_half], right.at[hi_half], g_send, g_recv.at[k, S_X2], down)
        to_sib(k, left)
        to_sib(k, right)

    def gather_last(k):
        mine = piece(k, core, xh, (y + 2) % 4)
        wait_recv(mine, g_recv.at[k, S_Y2])
        to_sib(k, mine)
        if k in BY_X:
            send(mine, mine, g_send, g_recv.at[k, S_X2], far)

    def gather_far_last(k):
        other = piece(k, core, 1 - xh, (y + 2) % 4)
        wait_recv(other, g_recv.at[k, S_X2])
        to_sib(k, other)

    def split(k):
        q = Q[k]
        wait_recv(rows(gath, 16 * OFF[k] + (1 - core) * 8 * q, 8 * q), g_recv.at[k, S_SIB])
        for core_ in range(2):
            for m in range(8):
                block = rows(gath, 16 * OFF[k] + (core_ * 8 + m) * q, q)[...]
                high = block.astype(BF16)
                low = (block - high.astype(F32)).astype(BF16)
                for t in range(2):
                    j = (2 * m + core_) * 2 + t
                    vals[j, 0:q] = high[:, t * BLK : (t + 1) * BLK]
                    vals[j, q : 2 * q] = low[:, t * BLK : (t + 1) * BLK]

    R_A, R_N, R_X = 0, 2, 4
    sides = (1 - xl, xl)

    def part_at(k, xl_, z_):
        return rows(part, (k % SLOTS) * 8 * QMAX + (xl_ * 4 + z_) * Q[k], Q[k])

    def got_a_at(k, g, side, count=1):
        return rows(got_a, 2 * OFF[k] + (g * 2 + side) * (Q[k] // 2), count * (Q[k] // 2))

    def got_n_at(k, g, side, count=1):
        return rows(got_n, 4 * OFF[k] + (g * 2 + side) * Q[k], count * Q[k])

    def multiply(k, lo, hi):
        q = Q[k]

        @pl.loop(lo, hi)
        def _(i):
            for u in range(UNROLL):
                g = i * UNROLL + u
                p0, p1 = idx[0, 2 * g], idx[0, 2 * g + 1]
                c0, c1 = idx[1, 2 * g], idx[1, 2 * g + 1]
                d = jnp.dot(vals[c0, 0 : 2 * q], tiles[p0], preferred_element_type=F32) + jnp.dot(
                    vals[c1, 0 : 2 * q], tiles[p1], preferred_element_type=F32
                )
                keep = idx[2, g].astype(F32)
                sums[g + 1, 0:q] = sums[g, 0:q] * keep + (d[:q] + d[q:])

    def send_n(k, g, half_up, half_down):
        ssem = r_send.at[k % SLOTS]
        n_up, n_down = part_at(k, sides[g], (z + 1) % 4), part_at(k, sides[g], (z + 3) % 4)
        to_up, to_down = (corner_up, corner_down) if k in CORNER and g == 0 else (zup, zdown)
        send(n_up.at[half_up], got_n_at(k, g, 0).at[half_up], ssem, r_recv.at[k, R_N + g], to_up)
        send(n_down.at[half_down], got_n_at(k, g, 1).at[half_down], ssem, r_recv.at[k, R_N + g], to_down)

    def send_a(k, g):
        ssem = r_send.at[k % SLOTS]
        lo_half, hi_half = halves(k)
        a = part_at(k, sides[g], (z + 2) % 4)
        send(a.at[lo_half], got_a_at(k, g, 0), ssem, r_recv.at[k, R_A + g], zup)
        send(a.at[hi_half], got_a_at(k, g, 1), ssem, r_recv.at[k, R_A + g], zdown)

    def reduce_start(k):
        q = Q[k]
        lo_half, hi_half = halves(k)
        if k >= SLOTS:
            wait_send(rows(part, 0, 7 * Q[k - SLOTS]), r_send.at[k % SLOTS])
        base = (k % SLOTS) * 8 * QMAX
        for i in range(16):
            at = base + (i // 2) * q
            part[at : at + q, (i % 2) * BLK : (i % 2 + 1) * BLK] = sums[idx[3, i], 0:q]
        if k in X_FIRST:
            a = part_at(k, 1 - xl, (z + 2) % 4)
            send(a, rows(got_f, OFF[k], q), r_send.at[k % SLOTS], r_recv.at[k, R_A], near)
            send_n(k, 0, pl.ds(0, q), pl.ds(0, q))
        else:
            send_a(k, 0)
            send_a(k, 1)
            send_n(k, 0, hi_half, lo_half)
        if k in CORNER:
            send(part_at(k, 1 - xl, z), rows(got_x, OFF[k], q), r_send.at[k % SLOTS], r_recv.at[k, R_X], near)

    def reduce_first(k):
        lo_half, hi_half = halves(k)
        got = rows(got_f, OFF[k], Q[k])
        wait_recv(got, r_recv.at[k, R_A])
        a = part_at(k, xl, (z + 2) % 4)
        a[...] = a[...] + got[...]
        send_a(k, 1)
        send_n(k, 1, hi_half, lo_half)

    def reduce_pass(k, g):
        h = Q[k] // 2
        lo_half, hi_half = halves(k)
        wait_recv(got_a_at(k, g, 0, 2), r_recv.at[k, R_A + g])
        n_up, n_down = part_at(k, sides[g], (z + 1) % 4), part_at(k, sides[g], (z + 3) % 4)
        n_up[0:h] = n_up[0:h] + got_a_at(k, g, 0)[...]
        n_down[h : 2 * h] = n_down[h : 2 * h] + got_a_at(k, g, 1)[...]
        send_n(k, g, lo_half, hi_half)
        if g == 0:
            send_n(k, 1, hi_half, lo_half)

    def reduce_two(k):
        wait_recv(got_n_at(k, 0, 0, 2), r_recv.at[k, R_N])
        mine = part_at(k, 1 - xl, z)
        mine[...] = mine[...] + got_n_at(k, 0, 0)[...] + got_n_at(k, 0, 1)[...]
        send(mine, rows(got_x, OFF[k], Q[k]), r_send.at[k % SLOTS], r_recv.at[k, R_X], near)

    def reduce_end(k):
        got = rows(got_x, OFF[k], Q[k])
        wait_recv(got_n_at(k, 1, 0, 2), r_recv.at[k, R_N + 1])
        wait_recv(got, r_recv.at[k, R_X])
        mine = part_at(k, xl, z)
        total = mine[...] + got_n_at(k, 1, 0)[...] + got_n_at(k, 1, 1)[...] + got[...]
        if k in CORNER:
            wait_recv(got_n_at(k, 0, 0, 2), r_recv.at[k, R_N])
            total = total + got_n_at(k, 0, 0)[...] + got_n_at(k, 0, 1)[...]
        center, radius = cen_ref[0], rad_ref[0]
        cols_at = pl.ds(OFF[k % NCH], Q[k])
        start = x_t[cols_at]
        if k < NCH:
            piece(k + NCH, core, xh, y)[...] = (total - center * start) / radius
        else:
            first = piece(k, core, xh, y)[...]
            o_t[cols_at] = 2.0 * (total - center * first) / radius - start

    x_copy.wait()
    x_t[...] = x_v[...].T
    for j in range(NCH):
        piece(j, core, xh, y)[...] = x_t[OFF[j] : OFF[j] + Q[j]]
    pl.semaphore_wait(barrier, len(others))

    gather_own(0)
    gather_own(1)

    ivec[...] = jnp.full(ivec.shape, 99, jnp.int32)
    ivec[0:1, 0:NT] = rows_ref[...]
    ivec[1:2, 0:NT] = cols_ref[...]
    lanes = lax.broadcasted_iota(jnp.int32, (1, 256), 1)
    row_of = jnp.where(lanes < live_ref[0], ivec[0:1], 99)
    row_l = jnp.broadcast_to(row_of, (256, 256))
    row_s = row_l.T
    col_s = jnp.broadcast_to(ivec[1:2], (256, 256)).T
    li = lax.broadcasted_iota(jnp.int32, (256, 256), 1)
    si = lax.broadcasted_iota(jnp.int32, (256, 256), 0)

    def count(mask, value=1, axis=1):
        return jnp.sum(jnp.where(mask, value, 0), axis=axis, keepdims=True)

    within = count((row_l == row_s) & (li < si))
    pairs = (count(row_s == li, axis=0) + 1) >> 1
    before = count(li < row_s, pairs)
    pairs_s = count(li == row_s, pairs)
    live = row_s < 16
    place = live & (2 * before + within == li)
    leads = live & (within == 0)
    ivec[0:1] = count(place, si, 0)
    ivec[1:2] = count(place, col_s - 32, 0) + 32
    ivec[2:3] = 1 - count(leads & (before == li), 1, 0)
    ivec[3:4] = count(leads & (row_s <= li), pairs_s, 0)
    to_smem = pltpu.make_async_copy(ivec, idx, i_sem)
    to_smem.start()

    def turn(i):
        tile_copy(i).wait()

        @pl.loop(0, per // 6)
        def _(s):
            for u in range(6):
                at = i * per + s * 6 + u
                tiles[at] = tiles[at].T

    vals[32] = jnp.zeros((2 * QMAX, BLK), BF16)
    sums[0] = jnp.zeros((QMAX, BLK), F32)

    step = {
        "own": gather_own, "far": gather_far, "ring": gather_ring, "far_ring": gather_far_ring,
        "last": gather_last, "far_last": gather_far_last, "split": split, "start": reduce_start,
        "first": reduce_first, "pass0": lambda k: reduce_pass(k, 0), "pass1": lambda k: reduce_pass(k, 1),
        "cross": reduce_two, "end": reduce_end, "turn": turn,
    }
    multiplied = 0
    for name, k, *span in ORDER:
        if name == "mul":
            if multiplied == 0 and k == 0:
                to_smem.wait()
                multiplied = 1
            multiply(k, *span)
        else:
            step[name](k)

    wait_send(rows(gath, 0, 15 * 2 * K), g_send)
    for k in range(STAGES - SLOTS, STAGES):
        wait_send(rows(part, 0, 7 * Q[k]), r_send.at[k % SLOTS])
    o_ref[...] = o_t[...].T


def local(start_basis, affinity_tiles, tile_rows, tile_cols, live_tiles, filter_center, filter_radius):
    vmem = pl.BlockSpec(memory_space=pltpu.VMEM)
    smem = pl.BlockSpec(memory_space=pltpu.SMEM)
    return pl.pallas_call(
        filter_kernel,
        name="chebyshev_filter",
        out_shape=jax.ShapeDtypeStruct((PIECE, K), F32),
        in_specs=[pl.BlockSpec(memory_space=pl.ANY), pl.BlockSpec(memory_space=pl.ANY), vmem, vmem, smem, smem, smem],
        out_specs=vmem,
        scratch_shapes=[
            pltpu.VMEM((NT, BLK, BLK), BF16),
            pltpu.VMEM((16 * 2 * K, PIECE), F32),
            pltpu.VMEM((33, 2 * QMAX, BLK), BF16),
            pltpu.VMEM((GROUPS + 1, QMAX, BLK), F32),
            pltpu.VMEM((SLOTS * 8 * QMAX, PIECE), F32),
            pltpu.VMEM((2 * 2 * K, PIECE), F32),
            pltpu.VMEM((4 * 2 * K, PIECE), F32),
            pltpu.VMEM((2 * K, PIECE), F32),
            pltpu.VMEM((2 * K, PIECE), F32),
            pltpu.VMEM((PIECE, K), F32),
            pltpu.VMEM((K, PIECE), F32),
            pltpu.VMEM((K, PIECE), F32),
            pltpu.VMEM((8, 256), jnp.int32),
            pltpu.SMEM((8, 256), jnp.int32),
            pltpu.SemaphoreType.DMA,
            pltpu.SemaphoreType.DMA((PARTS,)),
            pltpu.SemaphoreType.DMA,
            pltpu.SemaphoreType.DMA,
            pltpu.SemaphoreType.DMA((STAGES, 8)),
            pltpu.SemaphoreType.DMA((SLOTS,)),
            pltpu.SemaphoreType.DMA((STAGES, 5)),
        ],
        compiler_params=pltpu.CompilerParams(
            collective_id=0, has_side_effects=True, vmem_limit_bytes=60 * 2**20
        ),
        cost_estimate=pl.CostEstimate(
            flops=4 * NT * BLK * BLK * K * 2, bytes_accessed=NT * BLK * BLK * 2, transcendentals=0
        ),
    )(
        start_basis, affinity_tiles, tile_rows.reshape(1, NT), tile_cols.reshape(1, NT),
        live_tiles, filter_center, filter_radius,
    )


def solution(mesh):
    return jax.shard_map(
        local,
        mesh=mesh,
        in_specs=(
            P(("row", "col"), None),
            P(("row", "col"), None, None),
            P(("row", "col")),
            P(("row", "col")),
            P(("row", "col")),
            P(),
            P(),
        ),
        out_specs=P(("row", "col"), None),
        check_vma=False,
    )
```

```python
import functools

import jax
import jax.numpy as jnp
from jax import lax
from jax.experimental import pallas as pl
from jax.experimental.pallas import tpu as pltpu
from jax.sharding import PartitionSpec as P

MESH = pl.DeviceIdType.MESH
F32 = jnp.float32
BF16 = jnp.bfloat16
BLK = 256
NT = 144
PIECE = 512
K = 256
CHUNKS = (48, 48, 48, 64, 48)
NCH = len(CHUNKS)
STAGES = 2 * NCH
Q = CHUNKS + CHUNKS
QMAX = max(CHUNKS)
OFF = tuple(sum(Q[:k]) for k in range(STAGES))
GROUPS = 80
UNROLL = 16
PARTS = 8
SLOTS = 4
BY_X = (0, 1, 2, 3, 4)
DIRECT = ()
CORNER = ()
X_FIRST = (8, 9)
ORDER = (
    ("turn", 0), ("turn", 1), ("ring", 0), ("turn", 2), ("own", 2), ("turn", 3), ("ring", 1), ("far", 0),
    ("far", 1), ("turn", 4), ("last", 0), ("turn", 5), ("turn", 6), ("ring", 2), ("last", 1), ("own", 3),
    ("far_ring", 0), ("far_last", 0), ("own", 4), ("far", 2), ("turn", 7), ("split", 0), ("mul", 0, 0, 1),
    ("far_ring", 1), ("mul", 0, 1, 3), ("last", 2), ("far_last", 1), ("mul", 0, 3, 4), ("ring", 3),
    ("mul", 0, 4, 5), ("start", 0), ("split", 1), ("mul", 1, 0, 2), ("far", 3), ("mul", 1, 2, 3),
    ("far_ring", 2), ("ring", 4), ("far_last", 2), ("pass0", 0), ("far", 4), ("last", 3), ("mul", 1, 3, 5),
    ("start", 1), ("split", 2), ("mul", 2, 0, 1), ("pass1", 0), ("cross", 0), ("mul", 2, 1, 3), ("last", 4),
    ("far_ring", 3), ("far_last", 3), ("pass0", 1), ("mul", 2, 3, 5), ("start", 2), ("split", 3), ("end", 0),
    ("own", 5), ("mul", 3, 0, 1), ("far_ring", 4), ("mul", 3, 1, 2), ("cross", 1), ("pass1", 1),
    ("mul", 3, 2, 3), ("pass0", 2), ("mul", 3, 3, 4), ("far_last", 4), ("pass1", 2), ("far", 5),
    ("mul", 3, 4, 5), ("start", 3), ("ring", 5), ("split", 4), ("cross", 2), ("end", 1), ("mul", 4, 0, 1),
    ("own", 6), ("mul", 4, 1, 3), ("pass0", 3), ("far_ring", 5), ("mul", 4, 3, 4), ("end", 2), ("own", 7),
    ("mul", 4, 4, 5), ("start", 4), ("last", 5), ("far", 6), ("far_last", 5), ("cross", 3), ("pass1", 3),
    ("split", 5), ("ring", 6), ("mul", 5, 0, 1), ("ring", 7), ("pass0", 4), ("mul", 5, 1, 2), ("far_ring", 6),
    ("pass1", 4), ("mul", 5, 2, 3), ("far", 7), ("end", 3), ("own", 8), ("mul", 5, 3, 4), ("last", 6),
    ("last", 7), ("cross", 4), ("far_last", 6), ("mul", 5, 4, 5), ("start", 5), ("split", 6),
    ("mul", 6, 0, 1), ("far_ring", 7), ("mul", 6, 1, 2), ("far", 8), ("mul", 6, 2, 3), ("ring", 8),
    ("end", 4), ("own", 9), ("pass0", 5), ("mul", 6, 3, 4), ("far_last", 7), ("mul", 6, 4, 5), ("start", 6),
    ("pass1", 5), ("split", 7), ("mul", 7, 0, 1), ("far_ring", 8), ("cross", 5), ("far", 9), ("mul", 7, 1, 2),
    ("last", 8), ("mul", 7, 2, 3), ("ring", 9), ("pass0", 6), ("mul", 7, 3, 4), ("far_last", 8),
    ("mul", 7, 4, 5), ("start", 7), ("split", 8), ("end", 5), ("pass1", 6), ("far_ring", 9), ("mul", 8, 0, 1),
    ("last", 9), ("mul", 8, 1, 4), ("cross", 6), ("pass0", 7), ("far_last", 9), ("mul", 8, 4, 5),
    ("start", 8), ("split", 9), ("mul", 9, 0, 1), ("pass1", 7), ("mul", 9, 1, 5), ("start", 9), ("first", 8),
    ("cross", 8), ("first", 9), ("cross", 7), ("pass1", 8), ("end", 6), ("cross", 9), ("pass1", 9),
    ("end", 8), ("end", 7), ("end", 9),
)


def filter_kernel(
    x_ref, t_hbm, rows_ref, cols_ref, live_ref, cen_ref, rad_ref, o_ref,
    tiles, gath, vals, sums, part, got_a, got_n, got_x, got_f, x_v, x_t, o_t, ivec, idx,
    x_sem, t_sem, i_sem, g_send, g_recv, r_send, r_recv,
):
    row = lax.axis_index("row")
    col = lax.axis_index("col")
    xl, z = row // 4, row % 4
    xh, y, core = col // 8, (col // 2) % 4, col % 2

    def dev(xh_, xl_, y_, z_, core_):
        return (xl_ * 4 + z_, xh_ * 8 + y_ * 2 + core_)

    up, down = dev(xh, xl, (y + 1) % 4, z, core), dev(xh, xl, (y + 3) % 4, z, core)
    zup, zdown = dev(xh, xl, y, (z + 1) % 4, core), dev(xh, xl, y, (z + 3) % 4, core)
    sib = dev(xh, xl, y, z, 1 - core)
    far = dev(1 - xh, xl, y, z, core)
    near = dev(xh, 1 - xl, y, z, core)
    corner_up, corner_down = dev(xh, 1 - xl, y, (z + 1) % 4, core), dev(xh, 1 - xl, y, (z + 3) % 4, core)
    opposite, far_opposite = dev(xh, xl, (y + 2) % 4, z, core), dev(1 - xh, xl, (y + 2) % 4, z, core)
    far_up, far_down = dev(1 - xh, xl, (y + 1) % 4, z, core), dev(1 - xh, xl, (y + 3) % 4, z, core)

    x_copy = pltpu.make_async_copy(x_ref, x_v, x_sem)
    x_copy.start()
    barrier = pltpu.get_barrier_semaphore()
    others = (up, down, zup, zdown, sib, far, near)
    if CORNER:
        others += (corner_up, corner_down)
    if DIRECT:
        others += (opposite, far_opposite, far_up, far_down)
    for other in others:
        pl.semaphore_signal(barrier, inc=1, device_id=other, device_id_type=MESH)

    per = NT // PARTS

    def tile_copy(i):
        span = pl.ds(i * per, per)
        return pltpu.make_async_copy(t_hbm.at[span], tiles.at[span], t_sem.at[i])

    for i in range(PARTS):
        tile_copy(i).start()

    def send(src, dst, ssem, rsem, to):
        pltpu.make_async_remote_copy(
            src_ref=src, dst_ref=dst, send_sem=ssem, recv_sem=rsem, device_id=to, device_id_type=MESH
        ).start()

    def wait_recv(ref, sem):
        pltpu.make_async_remote_copy(
            src_ref=ref, dst_ref=ref, send_sem=g_send, recv_sem=sem, device_id=sib, device_id_type=MESH
        ).wait_recv()

    def wait_send(ref, sem):
        pltpu.make_async_remote_copy(
            src_ref=ref, dst_ref=ref, send_sem=sem, recv_sem=g_recv.at[0, 0], device_id=sib, device_id_type=MESH
        ).wait_send()

    def rows(ref, start, count):
        return ref.at[pl.ds(start if isinstance(start, int) else pl.multiple_of(start, 16), count)]

    def piece(k, core_, xh_, y_):
        return rows(gath, 16 * OFF[k] + (core_ * 8 + xh_ * 4 + y_) * Q[k], Q[k])

    def halves(k):
        return pl.ds(0, Q[k] // 2), pl.ds(Q[k] // 2, Q[k] // 2)

    S_L, S_R, S_X, S_Y2, S_XL, S_XR, S_X2, S_SIB = range(8)

    def to_sib(k, ref):
        send(ref, ref, g_send, g_recv.at[k, S_SIB], sib)

    def gather_own(k):
        own = piece(k, core, xh, y)
        send(own, own, g_send, g_recv.at[k, S_L], up)
        send(own, own, g_send, g_recv.at[k, S_R], down)
        send(own, own, g_send, g_recv.at[k, S_X], far)
        to_sib(k, own)
        if k in DIRECT:
            send(own, own, g_send, g_recv.at[k, S_Y2], opposite)
            send(own, own, g_send, g_recv.at[k, S_XL], far_up)
            send(own, own, g_send, g_recv.at[k, S_XR], far_down)
            send(own, own, g_send, g_recv.at[k, S_X2], far_opposite)

    def gather_far(k):
        opp = piece(k, core, 1 - xh, y)
        wait_recv(opp, g_recv.at[k, S_X])
        if k not in DIRECT:
            send(opp, opp, g_send, g_recv.at[k, S_XL], up)
            send(opp, opp, g_send, g_recv.at[k, S_XR], down)
        to_sib(k, opp)

    def gather_ring(k):
        left, right = piece(k, core, xh, (y + 3) % 4), piece(k, core, xh, (y + 1) % 4)
        lo_half, hi_half = halves(k)
        wait_recv(left, g_recv.at[k, S_L])
        if k not in DIRECT:
            send(left.at[lo_half], left.at[lo_half], g_send, g_recv.at[k, S_Y2], up)
        wait_recv(right, g_recv.at[k, S_R])
        if k not in DIRECT:
            send(right.at[hi_half], right.at[hi_half], g_send, g_recv.at[k, S_Y2], down)
        to_sib(k, left)
        to_sib(k, right)

    def gather_far_ring(k):
        left, right = piece(k, core, 1 - xh, (y + 3) % 4), piece(k, core, 1 - xh, (y + 1) % 4)
        lo_half, hi_half = halves(k)
        wait_recv(left, g_recv.at[k, S_XL])
        wait_recv(right, g_recv.at[k, S_XR])
        if k not in BY_X and k not in DIRECT:
            send(left.at[lo_half], left.at[lo_half], g_send, g_recv.at[k, S_X2], up)
            send(right.at[hi_half], right.at[hi_half], g_send, g_recv.at[k, S_X2], down)
        to_sib(k, left)
        to_sib(k, right)

    def gather_last(k):
        mine = piece(k, core, xh, (y + 2) % 4)
        wait_recv(mine, g_recv.at[k, S_Y2])
        to_sib(k, mine)
        if k in BY_X:
            send(mine, mine, g_send, g_recv.at[k, S_X2], far)

    def gather_far_last(k):
        other = piece(k, core, 1 - xh, (y + 2) % 4)
        wait_recv(other, g_recv.at[k, S_X2])
        to_sib(k, other)

    def split(k):
        q = Q[k]
        wait_recv(rows(gath, 16 * OFF[k] + (1 - core) * 8 * q, 8 * q), g_recv.at[k, S_SIB])
        for core_ in range(2):
            for m in range(8):
                block = rows(gath, 16 * OFF[k] + (core_ * 8 + m) * q, q)[...]
                high = block.astype(BF16)
                low = (block - high.astype(F32)).astype(BF16)
                for t in range(2):
                    j = (2 * m + core_) * 2 + t
                    vals[j, 0:q] = high[:, t * BLK : (t + 1) * BLK]
                    vals[j, q : 2 * q] = low[:, t * BLK : (t + 1) * BLK]

    R_A, R_N, R_X = 0, 2, 4
    sides = (1 - xl, xl)

    def part_at(k, xl_, z_):
        return rows(part, (k % SLOTS) * 8 * QMAX + (xl_ * 4 + z_) * Q[k], Q[k])

    def got_a_at(k, g, side, count=1):
        return rows(got_a, 2 * OFF[k] + (g * 2 + side) * (Q[k] // 2), count * (Q[k] // 2))

    def got_n_at(k, g, side, count=1):
        return rows(got_n, 4 * OFF[k] + (g * 2 + side) * Q[k], count * Q[k])

    def multiply(k, lo, hi):
        q = Q[k]

        @pl.loop(lo, hi)
        def _(i):
            for u in range(UNROLL):
                g = i * UNROLL + u
                p0, p1 = idx[0, 2 * g], idx[0, 2 * g + 1]
                c0, c1 = idx[1, 2 * g], idx[1, 2 * g + 1]
                d = jnp.dot(vals[c0, 0 : 2 * q], tiles[p0], preferred_element_type=F32) + jnp.dot(
                    vals[c1, 0 : 2 * q], tiles[p1], preferred_element_type=F32
                )
                keep = idx[2, g].astype(F32)
                sums[g + 1, 0:q] = sums[g, 0:q] * keep + (d[:q] + d[q:])

    def send_n(k, g, half_up, half_down):
        ssem = r_send.at[k % SLOTS]
        n_up, n_down = part_at(k, sides[g], (z + 1) % 4), part_at(k, sides[g], (z + 3) % 4)
        to_up, to_down = (corner_up, corner_down) if k in CORNER and g == 0 else (zup, zdown)
        send(n_up.at[half_up], got_n_at(k, g, 0).at[half_up], ssem, r_recv.at[k, R_N + g], to_up)
        send(n_down.at[half_down], got_n_at(k, g, 1).at[half_down], ssem, r_recv.at[k, R_N + g], to_down)

    def send_a(k, g):
        ssem = r_send.at[k % SLOTS]
        lo_half, hi_half = halves(k)
        a = part_at(k, sides[g], (z + 2) % 4)
        send(a.at[lo_half], got_a_at(k, g, 0), ssem, r_recv.at[k, R_A + g], zup)
        send(a.at[hi_half], got_a_at(k, g, 1), ssem, r_recv.at[k, R_A + g], zdown)

    def reduce_start(k):
        q = Q[k]
        lo_half, hi_half = halves(k)
        if k >= SLOTS:
            wait_send(rows(part, 0, 7 * Q[k - SLOTS]), r_send.at[k % SLOTS])
        base = (k % SLOTS) * 8 * QMAX
        for i in range(16):
            at = base + (i // 2) * q
            part[at : at + q, (i % 2) * BLK : (i % 2 + 1) * BLK] = sums[idx[3, i], 0:q]
        if k in X_FIRST:
            a = part_at(k, 1 - xl, (z + 2) % 4)
            send(a, rows(got_f, OFF[k], q), r_send.at[k % SLOTS], r_recv.at[k, R_A], near)
            send_n(k, 0, pl.ds(0, q), pl.ds(0, q))
        else:
            send_a(k, 0)
            send_a(k, 1)
            send_n(k, 0, hi_half, lo_half)
        if k in CORNER:
            send(part_at(k, 1 - xl, z), rows(got_x, OFF[k], q), r_send.at[k % SLOTS], r_recv.at[k, R_X], near)

    def reduce_first(k):
        lo_half, hi_half = halves(k)
        got = rows(got_f, OFF[k], Q[k])
        wait_recv(got, r_recv.at[k, R_A])
        a = part_at(k, xl, (z + 2) % 4)
        a[...] = a[...] + got[...]
        send_a(k, 1)
        send_n(k, 1, hi_half, lo_half)

    def reduce_pass(k, g):
        h = Q[k] // 2
        lo_half, hi_half = halves(k)
        wait_recv(got_a_at(k, g, 0, 2), r_recv.at[k, R_A + g])
        n_up, n_down = part_at(k, sides[g], (z + 1) % 4), part_at(k, sides[g], (z + 3) % 4)
        n_up[0:h] = n_up[0:h] + got_a_at(k, g, 0)[...]
        n_down[h : 2 * h] = n_down[h : 2 * h] + got_a_at(k, g, 1)[...]
        send_n(k, g, lo_half, hi_half)
        if g == 0:
            send_n(k, 1, hi_half, lo_half)

    def reduce_two(k):
        wait_recv(got_n_at(k, 0, 0, 2), r_recv.at[k, R_N])
        mine = part_at(k, 1 - xl, z)
        mine[...] = mine[...] + got_n_at(k, 0, 0)[...] + got_n_at(k, 0, 1)[...]
        send(mine, rows(got_x, OFF[k], Q[k]), r_send.at[k % SLOTS], r_recv.at[k, R_X], near)

    def reduce_end(k):
        got = rows(got_x, OFF[k], Q[k])
        wait_recv(got_n_at(k, 1, 0, 2), r_recv.at[k, R_N + 1])
        wait_recv(got, r_recv.at[k, R_X])
        mine = part_at(k, xl, z)
        total = mine[...] + got_n_at(k, 1, 0)[...] + got_n_at(k, 1, 1)[...] + got[...]
        if k in CORNER:
            wait_recv(got_n_at(k, 0, 0, 2), r_recv.at[k, R_N])
            total = total + got_n_at(k, 0, 0)[...] + got_n_at(k, 0, 1)[...]
        center, radius = cen_ref[0], rad_ref[0]
        cols_at = pl.ds(OFF[k % NCH], Q[k])
        start = x_t[cols_at]
        if k < NCH:
            piece(k + NCH, core, xh, y)[...] = (total - center * start) / radius
        else:
            first = piece(k, core, xh, y)[...]
            o_t[cols_at] = 2.0 * (total - center * first) / radius - start

    x_copy.wait()
    x_t[...] = x_v[...].T
    for j in range(NCH):
        piece(j, core, xh, y)[...] = x_t[OFF[j] : OFF[j] + Q[j]]
    pl.semaphore_wait(barrier, len(others))

    gather_own(0)
    gather_own(1)

    ivec[...] = jnp.full(ivec.shape, 99, jnp.int32)
    ivec[0:1, 0:NT] = rows_ref[...]
    ivec[1:2, 0:NT] = cols_ref[...]
    lanes = lax.broadcasted_iota(jnp.int32, (1, 256), 1)
    row_of = jnp.where(lanes < live_ref[0], ivec[0:1], 99)
    row_l = jnp.broadcast_to(row_of, (256, 256))
    row_s = row_l.T
    col_s = jnp.broadcast_to(ivec[1:2], (256, 256)).T
    li = lax.broadcasted_iota(jnp.int32, (256, 256), 1)
    si = lax.broadcasted_iota(jnp.int32, (256, 256), 0)

    def count(mask, value=1, axis=1):
        return jnp.sum(jnp.where(mask, value, 0), axis=axis, keepdims=True)

    within = count((row_l == row_s) & (li < si))
    pairs = (count(row_s == li, axis=0) + 1) >> 1
    before = count(li < row_s, pairs)
    pairs_s = count(li == row_s, pairs)
    live = row_s < 16
    place = live & (2 * before + within == li)
    leads = live & (within == 0)
    ivec[0:1] = count(place, si, 0)
    ivec[1:2] = count(place, col_s - 32, 0) + 32
    ivec[2:3] = 1 - count(leads & (before == li), 1, 0)
    ivec[3:4] = count(leads & (row_s <= li), pairs_s, 0)
    to_smem = pltpu.make_async_copy(ivec, idx, i_sem)
    to_smem.start()

    def turn(i):
        tile_copy(i).wait()

        @pl.loop(0, per // 6)
        def _(s):
            for u in range(6):
                at = i * per + s * 6 + u
                tiles[at] = tiles[at].T

    vals[32] = jnp.zeros((2 * QMAX, BLK), BF16)
    sums[0] = jnp.zeros((QMAX, BLK), F32)

    step = {
        "own": gather_own, "far": gather_far, "ring": gather_ring, "far_ring": gather_far_ring,
        "last": gather_last, "far_last": gather_far_last, "split": split, "start": reduce_start,
        "first": reduce_first, "pass0": lambda k: reduce_pass(k, 0), "pass1": lambda k: reduce_pass(k, 1),
        "cross": reduce_two, "end": reduce_end, "turn": turn,
    }
    multiplied = 0
    for name, k, *span in ORDER:
        if name == "mul":
            if multiplied == 0 and k == 0:
                to_smem.wait()
                multiplied = 1
            multiply(k, *span)
        else:
            step[name](k)

    wait_send(rows(gath, 0, 15 * 2 * K), g_send)
    for k in range(STAGES - SLOTS, STAGES):
        wait_send(rows(part, 0, 7 * Q[k]), r_send.at[k % SLOTS])
    o_ref[...] = o_t[...].T


def local(start_basis, affinity_tiles, tile_rows, tile_cols, live_tiles, filter_center, filter_radius):
    vmem = pl.BlockSpec(memory_space=pltpu.VMEM)
    smem = pl.BlockSpec(memory_space=pltpu.SMEM)
    return pl.pallas_call(
        filter_kernel,
        name="chebyshev_filter",
        out_shape=jax.ShapeDtypeStruct((PIECE, K), F32),
        in_specs=[pl.BlockSpec(memory_space=pl.ANY), pl.BlockSpec(memory_space=pl.ANY), vmem, vmem, smem, smem, smem],
        out_specs=vmem,
        scratch_shapes=[
            pltpu.VMEM((NT, BLK, BLK), BF16),
            pltpu.VMEM((16 * 2 * K, PIECE), F32),
            pltpu.VMEM((33, 2 * QMAX, BLK), BF16),
            pltpu.VMEM((GROUPS + 1, QMAX, BLK), F32),
            pltpu.VMEM((SLOTS * 8 * QMAX, PIECE), F32),
            pltpu.VMEM((2 * 2 * K, PIECE), F32),
            pltpu.VMEM((4 * 2 * K, PIECE), F32),
            pltpu.VMEM((2 * K, PIECE), F32),
            pltpu.VMEM((2 * K, PIECE), F32),
            pltpu.VMEM((PIECE, K), F32),
            pltpu.VMEM((K, PIECE), F32),
            pltpu.VMEM((K, PIECE), F32),
            pltpu.VMEM((8, 256), jnp.int32),
            pltpu.SMEM((8, 256), jnp.int32),
            pltpu.SemaphoreType.DMA,
            pltpu.SemaphoreType.DMA((PARTS,)),
            pltpu.SemaphoreType.DMA,
            pltpu.SemaphoreType.DMA,
            pltpu.SemaphoreType.DMA((STAGES, 8)),
            pltpu.SemaphoreType.DMA((SLOTS,)),
            pltpu.SemaphoreType.DMA((STAGES, 5)),
        ],
        compiler_params=pltpu.CompilerParams(
            collective_id=0, has_side_effects=True, vmem_limit_bytes=60 * 2**20
        ),
        cost_estimate=pl.CostEstimate(
            flops=4 * NT * BLK * BLK * K * 2, bytes_accessed=NT * BLK * BLK * 2, transcendentals=0
        ),
    )(
        start_basis, affinity_tiles, tile_rows.reshape(1, NT), tile_cols.reshape(1, NT),
        live_tiles, filter_center, filter_radius,
    )


def solution(mesh):
    return jax.shard_map(
        local,
        mesh=mesh,
        in_specs=(
            P(("row", "col"), None),
            P(("row", "col"), None, None),
            P(("row", "col")),
            P(("row", "col")),
            P(("row", "col")),
            P(),
            P(),
        ),
        out_specs=P(("row", "col"), None),
        check_vma=False,
    )
```
